32 devices in a mesh: groups: 2 (over x), ctx: 2 (over core), fsdp: 8 (over z, y).
Axes of the slice: x: 2, y: 2, z: 4, core: 2. Of those that a mesh axis runs over, the one named last changes fastest.
Arguments:
- hidden_in: bfloat16 [8192, 2048], P(('groups', 'ctx', 'fsdp')), parts along dimension 0, may hold values from -6 to 6
- qkv_weight: bfloat16 [2048, 4096], P(None, 'fsdp'), may hold values from -0.125 to 0.125
- ab_weight: bfloat16 [2048, 32], replicated, may hold values from -0.125 to 0.125
- conv_weight: float32 [4, 4096], replicated, may hold values from -3 to 3
- decay_rate: float32 [16], replicated, may hold values from 7.324219e-05 to 0.3
- dt_bias: float32 [16], replicated, may hold values from -3 to -1
- norm_gain: float32 [128], replicated, may hold values from 0.1 to 1.9
- previous_tail: bfloat16 [6, 4096], P('groups'), parts along dimension 0, may hold values from -6 to 6
- window_entry_state: float32 [32, 128, 128], P('groups'), parts along dimension 0, may hold values from -3 to 3
Outputs:
- head_out: bfloat16 [8192, 2048], P(('groups', 'ctx', 'fsdp')), parts along dimension 0
The draws below stay inside these ranges and needn't reach their ends.
There are 2 independent parts, one for each index of `groups`. The reference program is written for one: setup_inputs(seed, part) draws one part's arguments, and reference() takes and returns one part's arrays. A program takes and returns all parts, laid end to end along the dimension named above; an argument that names none is the same for every part. Nothing has to cross between parts.
All inputs are finite; a program needn't handle non-finite values.
Results may differ from the reference program's by a relative error of at most 0.0065.
Values may be sent and summed in bfloat16 or wider, within the bound.
A program may use at most 320 MiB of HBM per device.

```python
import math
import jax
import jax.numpy as jnp
from jax import lax

D = 2048
HK = 8
HV = 16
DK = 128
DV = 128
SPAN = 64
KERNEL = 4
CONV = 4096
TOKENS = 4096


def draw_decay_rate(key, part):
    low_end = math.log(1.0 / TOKENS)
    high_end = math.log(0.3)
    exponent = jax.random.uniform(key, (HV,), jnp.float32, low_end, high_end)
    return jnp.exp(exponent)


def levels(key, shape, shards, smallest, high):
    gain, own = 1.0, jax.random.fold_in(key, 6)
    for axis_at, blocks in shards:
        steps = jnp.exp(jax.random.uniform(jax.random.fold_in(own, axis_at), (blocks,), jnp.float32, smallest / len(shards), high / len(shards)))
        gain = gain * jnp.repeat(steps, shape[axis_at] // blocks).reshape([-1 if axis == axis_at else 1 for axis in range(len(shape))])
    return gain


def scatter_about(rng, shape, spread, most, shards=(), held_as=jnp.bfloat16):
    level = levels(rng, shape, shards, -0.22, 0.18) if shards else 1.0
    entries = jax.random.normal(rng, shape, jnp.float32) * spread * level
    return jnp.minimum(jnp.maximum(entries, -most), most).astype(held_as)


def setup_inputs(seed: int = 0, part: int = 0) -> dict:
    key_of = jax.random.split(jax.random.key(seed), 10)
    part_keys = jax.random.split(jax.random.fold_in(key_of[9], part), 10)
    return {
        "hidden_in": scatter_about(part_keys[0], (TOKENS, D), 1.0, 6.0, ((0, 16),)),
        "qkv_weight": scatter_about(key_of[1], (D, CONV), D ** -0.5, 0.125, ((1, 8),)),
        "ab_weight": scatter_about(key_of[2], (D, 2 * HV), D ** -0.5, 0.125),
        "conv_weight": scatter_about(key_of[3], (KERNEL, CONV), 0.5, 3.0, (), jnp.float32),
        "decay_rate": draw_decay_rate(jax.random.fold_in(key_of[9], 71), part),
        "dt_bias": jnp.clip(jax.random.uniform(key_of[5], (HV,), jnp.float32, -3.0, -1.0), -3.0, -1.0),
        "norm_gain": jnp.clip(1.0 + 0.18 * jax.random.normal(key_of[6], (DV,), jnp.float32), 0.1, 1.9),
        "previous_tail": scatter_about(part_keys[7], (KERNEL - 1, CONV), 1.0, 6.0),
        "window_entry_state": scatter_about(part_keys[8], (HV, DK, DV), 0.5, 3.0, (), jnp.float32),
    }


exact_product = lax.Precision.HIGHEST

def unit_norm(vectors):
    return vectors * lax.rsqrt(lax.optimization_barrier(jnp.sum(vectors * vectors, axis=-1, keepdims=True)) + 1e-06)

def convolve(before, mixed_qkv, conv_weight):
    length = mixed_qkv.shape[0]
    padded = jnp.concatenate([before, mixed_qkv], axis=0).astype(jnp.float32)
    summed = jnp.zeros((length, mixed_qkv.shape[1]), jnp.float32)
    for offset in range(conv_weight.shape[0]):
        summed = summed + conv_weight[offset] * padded[offset:offset + length]
    return jax.nn.silu(summed)

def to_spans(tensor, span_len):
    length, head_count = (tensor.shape[0], tensor.shape[1])
    shaped = tensor.reshape((length // span_len, span_len, head_count) + tensor.shape[2:])
    return jnp.moveaxis(shaped, 2, 1)

def head_inputs(conv_out, gate_logits, decay_rate, dt_bias):
    length = conv_out.shape[0]
    queries = unit_norm(conv_out[:, :HK * DK].reshape(length, HK, DK)) * DK ** (-0.5)
    head_keys = unit_norm(conv_out[:, HK * DK:2 * HK * DK].reshape(length, HK, DK))
    values = conv_out[:, 2 * HK * DK:].reshape(length, HV, DV)
    queries = jnp.repeat(queries, HV // HK, axis=1)
    head_keys = jnp.repeat(head_keys, HV // HK, axis=1)
    write_rate = jax.nn.sigmoid(gate_logits[:, HV:])
    logdecay = -decay_rate * jax.nn.softplus(gate_logits[:, :HV] + dt_bias)
    return [to_spans(item, SPAN) for item in (queries, head_keys, values, write_rate, logdecay)]

def lower_inverse(strict_part):
    span_len = strict_part.shape[-1]
    unit_span = jnp.eye(span_len, dtype=strict_part.dtype)
    inverse = unit_span - strict_part
    power = strict_part
    reach = 2
    while reach < span_len:
        power = jnp.einsum('...ij,...jk->...ik', power, power, precision=exact_product)
        inverse = inverse + jnp.einsum('...ij,...jk->...ik', inverse, power, precision=exact_product)
        reach = reach * 2
    return inverse

def span_terms(queries, head_keys, values, write_rate, logdecay):
    span_len = logdecay.shape[-1]
    cumulative = jnp.cumsum(logdecay, axis=-1)
    row_index = lax.broadcasted_iota(jnp.int32, (span_len, span_len), 0)
    col_index = lax.broadcasted_iota(jnp.int32, (span_len, span_len), 1)
    lower_mask = row_index >= col_index
    gap_log = cumulative[..., :, None] - cumulative[..., None, :]
    factor = jnp.where(lower_mask, jnp.exp(jnp.where(lower_mask, gap_log, 0.0)), 0.0)
    strict = jnp.where(row_index > col_index, factor, 0.0)
    key_products = jnp.einsum('...ik,...jk->...ij', head_keys, head_keys, precision=exact_product)
    query_products = jnp.einsum('...ik,...jk->...ij', queries, head_keys, precision=exact_product)
    inverse = lower_inverse(write_rate[..., :, None] * key_products * strict)
    growth = jnp.exp(cumulative)
    right_sides = jnp.concatenate([write_rate[..., None] * values, (write_rate * growth)[..., None] * head_keys], axis=-1)
    solved = jnp.einsum('...ij,...jc->...ic', inverse, right_sides, precision=exact_product)
    new_values = solved[..., :values.shape[-1]]
    key_weights = solved[..., values.shape[-1]:]
    scores = query_products * factor
    window_local_output = jnp.einsum('...ij,...jv->...iv', scores, new_values, precision=exact_product)
    effective_query = growth[..., None] * queries - jnp.einsum('...ij,...jk->...ik', scores, key_weights, precision=exact_product)
    span_end = cumulative[..., -1]
    tail_decay = jnp.exp(span_end[..., None] - cumulative)
    decayed_keys = head_keys * tail_decay[..., None]
    unit_key = jnp.eye(head_keys.shape[-1], dtype=logdecay.dtype)
    state_mapping = jnp.exp(span_end)[..., None, None] * unit_key - jnp.einsum('...ck,...cj->...kj', decayed_keys, key_weights, precision=exact_product)
    shifted_state = jnp.einsum('...ck,...cv->...kv', decayed_keys, new_values, precision=exact_product)
    return (effective_query, window_local_output, state_mapping, shifted_state)

def finish(result_rows, norm_gain):
    mean_square = lax.optimization_barrier(jnp.mean(result_rows * result_rows, axis=-1, keepdims=True))
    normed = result_rows * lax.rsqrt(mean_square + 1e-06) * norm_gain
    normed = jnp.moveaxis(normed, 1, 2)
    return normed.reshape(normed.shape[0] * normed.shape[1], normed.shape[2] * normed.shape[3]).astype(jnp.bfloat16)

def reference(hidden_in, qkv_weight, ab_weight, conv_weight, decay_rate, dt_bias, norm_gain, previous_tail, window_entry_state):
    mixed_qkv = jnp.dot(hidden_in, qkv_weight, preferred_element_type=jnp.float32).astype(jnp.bfloat16)
    gate_logits = jnp.dot(hidden_in, ab_weight, preferred_element_type=jnp.float32)
    conv_out = convolve(previous_tail, mixed_qkv, conv_weight)
    spanned = head_inputs(conv_out, gate_logits, decay_rate, dt_bias)

    def advance(carried_over_state, items):
        effective_query, window_local_output, state_mapping, shifted_state = span_terms(*items)
        layer_result = window_local_output + jnp.einsum('gpi,gib->gpb', effective_query, carried_over_state, precision=exact_product)
        carried_over_state = jnp.einsum('zom,zmg->zog', state_mapping, carried_over_state, precision=exact_product) + shifted_state
        return (carried_over_state, layer_result)
    final_state, result_rows = lax.scan(advance, window_entry_state, tuple(spanned))
    return finish(result_rows, norm_gain)
```

```python
import jax
import jax.numpy as jnp
from jax import lax
from jax.experimental import pallas as pl
from jax.experimental.pallas import tpu as pltpu
from jax.sharding import PartitionSpec as P

HK = 8
HV = 16
DK = 128
DV = 128
BLOCK = 512
CHUNK = 128
BASE = 32


def mm(a, b):
    return jnp.dot(a.astype(jnp.bfloat16), b.astype(jnp.bfloat16), preferred_element_type=jnp.float32)


def mm_nt(a, b):
    return lax.dot_general(
        a.astype(jnp.bfloat16),
        b.astype(jnp.bfloat16),
        (((1,), (1,)), ((), ())),
        preferred_element_type=jnp.float32,
    )


def mm_tn(a, b):
    return lax.dot_general(
        a.astype(jnp.bfloat16),
        b.astype(jnp.bfloat16),
        (((0,), (0,)), ((), ())),
        preferred_element_type=jnp.float32,
    )


def unit_lower_inverses(parts, row, col):
    eye = jnp.where(row == col, 1.0, 0.0)
    near = (row // BASE) == (col // BASE)
    powers = [jnp.where(near, a, 0.0) for a in parts]
    inverses = [eye - p for p in powers]
    reach = 2
    while reach < BASE:
        powers = [mm(p, p) for p in powers]
        inverses = [x + mm(x, p) for x, p in zip(inverses, powers)]
        reach *= 2
    size = BASE
    while size < CHUNK:
        joined = ((row // (2 * size)) == (col // (2 * size))) & ((row // size) != (col // size))
        sides = [mm(x, jnp.where(joined, a, 0.0)) for x, a in zip(inverses, parts)]
        inverses = [x - mm(y, x) for x, y in zip(inverses, sides)]
        size *= 2
    return inverses


def layer_kernel(hid_ref, w_ref, taps_ref, scal_ref, tail_ref, entry_ref, out_ref, buf, state):
    step = pl.program_id(0)

    @pl.when(step == 0)
    def _():
        state[...] = entry_ref[...]
        buf[0:8, :] = tail_ref[...]

    block = hid_ref.shape[0]
    wide = 3 * DK
    product = jnp.dot(hid_ref[...], w_ref[...], preferred_element_type=jnp.float32)
    buf[8 : 8 + block, :] = product[:, :wide].astype(jnp.bfloat16).astype(jnp.float32)
    summed = taps_ref[0:1, :] * buf[5 : 5 + block, :]
    for j in range(1, 4):
        summed = summed + taps_ref[j : j + 1, :] * buf[5 + j : 5 + j + block, :]
    buf[0:8, :] = buf[block : block + 8, :]
    conv = summed / (1.0 + jnp.exp(-summed))
    q = conv[:, :DK]
    k = conv[:, DK : 2 * DK]
    v = conv[:, 2 * DK :]
    q = q * (lax.rsqrt(jnp.sum(q * q, axis=-1, keepdims=True) + 1e-06) * DK ** (-0.5))
    k = k * lax.rsqrt(jnp.sum(k * k, axis=-1, keepdims=True) + 1e-06)

    spans = block // CHUNK
    row = lax.broadcasted_iota(jnp.int32, (CHUNK, CHUNK), 0)
    col = lax.broadcasted_iota(jnp.int32, (CHUNK, CHUNK), 1)
    low = row >= col
    upper = jnp.where(row <= col, 1.0, 0.0)
    logits = jnp.transpose(product[:, wide:], (1, 0))[0:8, :]
    shifted_logit = logits[0:1, :] + scal_ref[1:2, 0:1]
    softplus = jnp.maximum(shifted_logit, 0.0) + jnp.log1p(jnp.exp(-jnp.abs(shifted_logit)))
    logdecay = -scal_ref[0:1, 0:1] * softplus
    rate = 1.0 / (1.0 + jnp.exp(-logits[1:2, :]))
    decays = jnp.concatenate(
        [logdecay[:, i * CHUNK : (i + 1) * CHUNK] for i in range(spans)]
        + [jnp.zeros((8 - spans, CHUNK), jnp.float32)] * (1 if spans < 8 else 0),
        axis=0,
    )
    sums = jnp.dot(decays, upper, precision=lax.Precision.HIGHEST, preferred_element_type=jnp.float32)

    ks, qs, parts, scores, rights, ends, tails = [], [], [], [], [], [], []
    for i in range(spans):
        part = slice(i * CHUNK, (i + 1) * CHUNK)
        ki, qi, vi = k[part], q[part], v[part]
        cs = sums[i : i + 1, :]
        beta = rate[:, part]
        end = cs[:, CHUNK - 1 : CHUNK]
        growth = jnp.exp(cs)
        rows = jnp.concatenate(
            [cs, beta, growth, beta * growth, jnp.exp(end - cs), jnp.zeros((CHUNK - 5, CHUNK), jnp.float32)], axis=0
        )
        cols = jnp.transpose(rows, (1, 0))
        gap = cols[:, 0:1] - cs
        factor = jnp.where(low, jnp.exp(jnp.where(low, gap, 0.0)), 0.0)
        both = mm_nt(jnp.concatenate([ki, qi], axis=0), ki)
        parts.append(jnp.where(row > col, cols[:, 1:2] * both[:CHUNK] * factor, 0.0))
        scores.append(both[CHUNK:] * factor)
        rights.append(jnp.concatenate([cols[:, 1:2] * vi, cols[:, 3:4] * ki], axis=1))
        qs.append(cols[:, 2:3] * qi)
        ks.append(ki * cols[:, 4:5])
        ends.append(jnp.exp(end))
    inverses = unit_lower_inverses(parts, row, col)
    solved = [mm(x, r) for x, r in zip(inverses, rights)]

    held = state[...]
    for i in range(spans):
        both = mm(jnp.concatenate([solved[i][:, DV:], qs[i]], axis=0), held)
        fresh = solved[i][:, :DV] - both[:CHUNK]
        result = both[CHUNK:] + mm(scores[i], fresh)
        held = ends[i] * held + mm_tn(ks[i], fresh)
        mean_square = jnp.mean(result * result, axis=-1, keepdims=True)
        out_ref[i * CHUNK : (i + 1) * CHUNK, :] = (
            result * lax.rsqrt(mean_square + 1e-06) * scal_ref[2:3, :]
        ).astype(jnp.bfloat16)
    state[...] = held


def layer(hidden, weights, taps, scal, tail, entry, interpret=False):
    tokens, width = hidden.shape
    full = lambda a: pl.BlockSpec(a.shape, lambda i: (0,) * a.ndim)
    return pl.pallas_call(
        layer_kernel,
        grid=(tokens // BLOCK,),
        in_specs=[pl.BlockSpec((BLOCK, width), lambda i: (i, 0))]
        + [full(a) for a in (weights, taps, scal, tail, entry)],
        out_specs=pl.BlockSpec((BLOCK, DV), lambda i: (i, 0)),
        out_shape=jax.ShapeDtypeStruct((tokens, DV), jnp.bfloat16),
        scratch_shapes=[pltpu.VMEM((BLOCK + 8, 3 * DK), jnp.float32), pltpu.VMEM((DK, DV), jnp.float32)],
        compiler_params=pltpu.CompilerParams(vmem_limit_bytes=48 * 1024 * 1024),
        interpret=interpret,
    )(hidden, weights, taps, scal, tail, entry)


def head_columns(array, own_qk, own_v):
    picks = (own_qk * DK, (HK + own_qk) * DK, 2 * HK * DK + own_v * DV)
    return jnp.concatenate([lax.dynamic_slice_in_dim(array, at, DK, 1) for at in picks], axis=1)


def ring_member(place, peers):
    late = place // (peers // 2)
    return 2 * place * (1 - late) + (2 * peers - 1 - 2 * place) * late


def exchange_kernel(
    hid_ref, shard_ref, gate_ref, all_ref, w_ref, ring_send, ring_recv, twin_send, twin_recv, local, w_send, w_recv, w_local
):
    c, f = lax.axis_index("ctx"), lax.axis_index("fsdp")
    peers = HK
    rows = hid_ref.shape[0]
    half = rows // 2
    place = (f // 2) * (1 - f % 2) + (peers - 1 - f // 2) * (f % 2)
    there = lambda cc, ff: {"ctx": cc, "fsdp": ff}
    barrier = pltpu.get_barrier_semaphore()
    for cc in range(2):
        for df in range(peers):
            if cc or df:
                pl.semaphore_signal(
                    barrier,
                    inc=1,
                    device_id=there((c + cc) % 2, (f + df) % peers),
                    device_id_type=pl.DeviceIdType.MESH,
                )
    pl.semaphore_wait(barrier, 2 * peers - 1)

    def remote(src, dst, send, recv, device):
        return pltpu.make_async_remote_copy(
            src_ref=src, dst_ref=dst, send_sem=send, recv_sem=recv, device_id=device, device_id_type=pl.DeviceIdType.MESH
        )

    def landing(member, start, size):
        return all_ref.at[pl.ds(pl.multiple_of((c * peers + member) * rows + start, half), size), :]

    def span(way, hop):
        return (0, rows) if hop < peers // 2 else ((0, half) if way == 0 else (half, half))

    def ring(way, hop):
        ahead = 1 if way == 0 else peers - 1
        target = ring_member((place + ahead) % peers, peers)
        origin = ring_member((place + (peers - ahead) * (hop - 1)) % peers, peers)
        start, size = span(way, hop)
        src = hid_ref.at[pl.ds(start, size), :] if hop == 1 else landing(origin, start, size)
        return remote(
            src, landing(origin, start, size), ring_send.at[way, hop - 1], ring_recv.at[way, hop - 1], there(c, target)
        )

    def twin(way, hop):
        ahead = 1 if way == 0 else peers - 1
        origin = ring_member((place + (peers - ahead) * hop) % peers, peers)
        block = landing(origin, *span(way, hop))
        at = 1 + way * (peers // 2) + hop - 1
        return remote(block, block, twin_send.at[at], twin_recv.at[at], there(1 - c, f))

    halves = shard_ref.shape[0] // 2

    def weight(i, qk):
        if qk:
            d = (HK // 2) * (f % 2) + i
            lines = pl.ds(pl.multiple_of(c * halves, halves), halves)
            src = shard_ref.at[lines, pl.ds(i * DK, DK)]
            dst = w_ref.at[lines, pl.ds(pl.multiple_of((f // 2) * DK, DK), DK)]
            sem = w_recv.at[f // 2]
        else:
            d = 2 * (f - 4) + i
            src = shard_ref.at[:, pl.ds(pl.multiple_of((2 * i + c) * DK, DK), DK)]
            dst = w_ref.at[:, pl.ds(2 * DK, DK)]
            sem = w_recv.at[2]
        return d, src, dst, sem

    def weights(finish):
        for qk, count in ((True, 4), (False, 2)):

            @pl.when((f < 4) if qk else (f >= 4))
            def _():
                for i in range(count):
                    d, src, dst, sem = weight(i, qk)

                    @pl.when(d != f)
                    def _():
                        far = remote(src, dst, w_send.at[i], sem, there(c, d))
                        far.wait_send() if finish else far.start()

                    if not finish:

                        @pl.when(d == f)
                        def _():
                            pltpu.make_async_copy(src, dst, sem).start()

    def weight_twin(t):
        block = w_ref.at[pl.ds(pl.multiple_of(c * halves, halves), halves), pl.ds(t * DK, DK)]
        return remote(block, block, w_send.at[4 + t], w_recv.at[3 + t], there(1 - c, f))

    weights(False)
    hops = peers // 2
    for way in range(2):
        ring(way, 1).start()
    first = remote(hid_ref, landing(f, 0, rows), twin_send.at[0], twin_recv.at[0], there(1 - c, f))
    first.start()
    own = pltpu.make_async_copy(hid_ref, landing(f, 0, rows), local)
    own.start()
    gate = pltpu.make_async_copy(gate_ref, w_ref.at[:, pl.ds(3 * DK, DK)], w_local)
    gate.start()
    for hop in range(1, hops + 1):
        for way in range(2):
            ring(way, hop).wait_recv()
            if hop < hops:
                ring(way, hop + 1).start()
            twin(way, hop).start()
        if hop == 1:
            for t in range(2):
                block = w_ref.at[pl.ds(pl.multiple_of(c * halves, halves), halves), pl.ds(t * DK, DK)]
                pltpu.make_async_copy(block, block, w_recv.at[t]).wait()
                weight_twin(t).start()
    block = w_ref.at[:, pl.ds(2 * DK, DK)]
    pltpu.make_async_copy(block, block, w_recv.at[2]).wait()
    own.wait()
    gate.wait()
    first.wait()
    for t in range(2):
        weight_twin(t).wait()
    weights(True)
    for hop in range(1, hops + 1):
        for way in range(2):
            ring(way, hop).wait_send()
            twin(way, hop).wait()


def exchange(hidden_in, qkv_weight, gates):
    rows, width = hidden_in.shape
    anywhere = pl.BlockSpec(memory_space=pl.ANY)
    dma = pltpu.SemaphoreType.DMA
    return pl.pallas_call(
        exchange_kernel,
        in_specs=[anywhere] * 3,
        out_specs=[anywhere] * 2,
        out_shape=[
            jax.ShapeDtypeStruct((2 * HK * rows, width), jnp.bfloat16),
            jax.ShapeDtypeStruct((width, 4 * DK), jnp.bfloat16),
        ],
        scratch_shapes=[dma((2, HK // 2)), dma((2, HK // 2)), dma((HK + 1,)), dma((HK + 1,)), dma, dma((6,)), dma((5,)), dma],
        compiler_params=pltpu.CompilerParams(collective_id=0, has_side_effects=True),
    )(hidden_in, qkv_weight, gates)


def shards(
    hidden_in,
    qkv_weight,
    ab_weight,
    conv_weight,
    decay_rate,
    dt_bias,
    norm_gain,
    previous_tail,
    window_entry_state,
):
    c, f = lax.axis_index("ctx"), lax.axis_index("fsdp")
    own_qk = f % HK
    own = (HV // HK) * own_qk + c
    both = ("ctx", "fsdp")
    gates = jnp.stack(
        [lax.dynamic_index_in_dim(ab_weight, own, 1, False), lax.dynamic_index_in_dim(ab_weight, HV + own, 1, False)],
        axis=1,
    )
    gates = jnp.pad(gates, ((0, 0), (0, DK - 2)))
    if lax.axis_size("fsdp") == HK:
        hidden, weights = exchange(hidden_in, qkv_weight, gates)
    else:
        hidden = lax.all_gather(hidden_in, both, axis=0, tiled=True)
        columns = head_columns(lax.all_gather(qkv_weight, "fsdp", axis=1, tiled=True), own_qk, own)
        weights = jnp.concatenate([columns, gates], axis=1)
    taps = jnp.pad(head_columns(conv_weight, own_qk, own), ((0, 4), (0, 0)))
    tail = jnp.pad(head_columns(previous_tail, own_qk, own).astype(jnp.float32), ((5, 0), (0, 0)))
    take = lambda a: jnp.full((1, DV), lax.dynamic_index_in_dim(a, own, 0, False))
    scal = jnp.concatenate(
        [take(decay_rate), take(dt_bias), norm_gain[None, :], jnp.zeros((5, DV), jnp.float32)], axis=0
    )
    entry = lax.dynamic_index_in_dim(window_entry_state, own, 0, False)
    result = layer(hidden, weights, taps, scal, tail, entry)
    peers = lax.axis_size("ctx") * lax.axis_size("fsdp")
    rows = result.reshape(peers, result.shape[0] // peers, DV)
    swapped = lax.all_to_all(rows, both, 0, 0)
    swapped = swapped.reshape(lax.axis_size("ctx"), lax.axis_size("fsdp"), rows.shape[1], DV)[:, :HK]
    return jnp.transpose(swapped, (2, 1, 0, 3)).reshape(rows.shape[1], HV * DV)


def solution(mesh):
    placed = (
        P(("groups", "ctx", "fsdp"), None),
        P(None, "fsdp"),
        P(),
        P(),
        P(),
        P(),
        P(),
        P("groups", None),
        P("groups", None, None),
    )
    return jax.shard_map(
        shards,
        mesh=mesh,
        in_specs=placed,
        out_specs=P(("groups", "ctx", "fsdp"), None),
        check_vma=False,
    )
```

```python
import jax
import jax.numpy as jnp
from jax import lax
from jax.experimental import pallas as pl
from jax.experimental.pallas import tpu as pltpu
from jax.sharding import PartitionSpec as P

HK = 8
HV = 16
DK = 128
DV = 128
BLOCK = 512
CHUNK = 128
BASE = 32


def mm(a, b):
    return jnp.dot(a.astype(jnp.bfloat16), b.astype(jnp.bfloat16), preferred_element_type=jnp.float32)


def mm_nt(a, b):
    return lax.dot_general(
        a.astype(jnp.bfloat16),
        b.astype(jnp.bfloat16),
        (((1,), (1,)), ((), ())),
        preferred_element_type=jnp.float32,
    )


def mm_tn(a, b):
    return lax.dot_general(
        a.astype(jnp.bfloat16),
        b.astype(jnp.bfloat16),
        (((0,), (0,)), ((), ())),
        preferred_element_type=jnp.float32,
    )


def unit_lower_inverses(parts, row, col):
    eye = jnp.where(row == col, 1.0, 0.0)
    near = (row // BASE) == (col // BASE)
    powers = [jnp.where(near, a, 0.0) for a in parts]
    inverses = [eye - p for p in powers]
    reach = 2
    while reach < BASE:
        powers = [mm(p, p) for p in powers]
        inverses = [x + mm(x, p) for x, p in zip(inverses, powers)]
        reach *= 2
    size = BASE
    while size < CHUNK:
        joined = ((row // (2 * size)) == (col // (2 * size))) & ((row // size) != (col // size))
        sides = [mm(x, jnp.where(joined, a, 0.0)) for x, a in zip(inverses, parts)]
        inverses = [x - mm(y, x) for x, y in zip(inverses, sides)]
        size *= 2
    return inverses


def layer_kernel(hid_ref, w_ref, taps_ref, scal_ref, tail_ref, entry_ref, out_ref, buf, state, *sending):
    step = pl.program_id(0)
    if sending:
        held_out, send, recv = sending
        c, f = lax.axis_index("ctx"), lax.axis_index("fsdp")
        me, peers = c * HK + f, 2 * HK
        own = 2 * f + c
        share = out_ref.shape[0]
        barrier = pltpu.get_barrier_semaphore()

        @pl.when(step == 0)
        def _():
            for away in range(1, peers):
                other = (me + away) % peers
                pl.semaphore_signal(
                    barrier,
                    inc=1,
                    device_id={"ctx": other // HK, "fsdp": other % HK},
                    device_id_type=pl.DeviceIdType.MESH,
                )

    @pl.when(step == 0)
    def _():
        state[...] = entry_ref[...]
        buf[0:8, :] = tail_ref[...]

    block = hid_ref.shape[0]
    wide = 3 * DK
    product = jnp.dot(hid_ref[...], w_ref[...], preferred_element_type=jnp.float32)
    buf[8 : 8 + block, :] = product[:, :wide].astype(jnp.bfloat16).astype(jnp.float32)
    summed = taps_ref[0:1, :] * buf[5 : 5 + block, :]
    for j in range(1, 4):
        summed = summed + taps_ref[j : j + 1, :] * buf[5 + j : 5 + j + block, :]
    buf[0:8, :] = buf[block : block + 8, :]
    conv = summed / (1.0 + jnp.exp(-summed))
    q = conv[:, :DK]
    k = conv[:, DK : 2 * DK]
    v = conv[:, 2 * DK :]
    q = q * (lax.rsqrt(jnp.sum(q * q, axis=-1, keepdims=True) + 1e-06) * DK ** (-0.5))
    k = k * lax.rsqrt(jnp.sum(k * k, axis=-1, keepdims=True) + 1e-06)

    spans = block // CHUNK
    row = lax.broadcasted_iota(jnp.int32, (CHUNK, CHUNK), 0)
    col = lax.broadcasted_iota(jnp.int32, (CHUNK, CHUNK), 1)
    low = row >= col
    upper = jnp.where(row <= col, 1.0, 0.0)
    logits = jnp.transpose(product[:, wide:], (1, 0))[0:8, :]
    shifted_logit = logits[0:1, :] + scal_ref[1:2, 0:1]
    softplus = jnp.maximum(shifted_logit, 0.0) + jnp.log1p(jnp.exp(-jnp.abs(shifted_logit)))
    logdecay = -scal_ref[0:1, 0:1] * softplus
    rate = 1.0 / (1.0 + jnp.exp(-logits[1:2, :]))
    decays = jnp.concatenate(
        [logdecay[:, i * CHUNK : (i + 1) * CHUNK] for i in range(spans)]
        + [jnp.zeros((8 - spans, CHUNK), jnp.float32)] * (1 if spans < 8 else 0),
        axis=0,
    )
    sums = jnp.dot(decays, upper, precision=lax.Precision.HIGHEST, preferred_element_type=jnp.float32)

    ks, qs, parts, scores, rights, ends, tails = [], [], [], [], [], [], []
    for i in range(spans):
        part = slice(i * CHUNK, (i + 1) * CHUNK)
        ki, qi, vi = k[part], q[part], v[part]
        cs = sums[i : i + 1, :]
        beta = rate[:, part]
        end = cs[:, CHUNK - 1 : CHUNK]
        growth = jnp.exp(cs)
        rows = jnp.concatenate(
            [cs, beta, growth, beta * growth, jnp.exp(end - cs), jnp.zeros((CHUNK - 5, CHUNK), jnp.float32)], axis=0
        )
        cols = jnp.transpose(rows, (1, 0))
        gap = cols[:, 0:1] - cs
        factor = jnp.where(low, jnp.exp(jnp.where(low, gap, 0.0)), 0.0)
        both = mm_nt(jnp.concatenate([ki, qi], axis=0), ki)
        parts.append(jnp.where(row > col, cols[:, 1:2] * both[:CHUNK] * factor, 0.0))
        scores.append(both[CHUNK:] * factor)
        rights.append(jnp.concatenate([cols[:, 1:2] * vi, cols[:, 3:4] * ki], axis=1))
        qs.append(cols[:, 2:3] * qi)
        ks.append(ki * cols[:, 4:5])
        ends.append(jnp.exp(end))
    inverses = unit_lower_inverses(parts, row, col)
    solved = [mm(x, r) for x, r in zip(inverses, rights)]

    held = state[...]
    for i in range(spans):
        both = mm(jnp.concatenate([solved[i][:, DV:], qs[i]], axis=0), held)
        fresh = solved[i][:, :DV] - both[:CHUNK]
        result = both[CHUNK:] + mm(scores[i], fresh)
        held = ends[i] * held + mm_tn(ks[i], fresh)
        mean_square = jnp.mean(result * result, axis=-1, keepdims=True)
        normed = (result * lax.rsqrt(mean_square + 1e-06) * scal_ref[2:3, :]).astype(jnp.bfloat16)
        if sending:
            held_out[pl.ds(pl.multiple_of(step * block + i * CHUNK, CHUNK), CHUNK), :] = normed
        else:
            out_ref[i * CHUNK : (i + 1) * CHUNK, :] = normed
    state[...] = held
    if not sending:
        return

    @pl.when(step == 0)
    def _():
        pl.semaphore_wait(barrier, peers - 1)

    def leave(other):
        return pltpu.make_async_remote_copy(
            src_ref=held_out.at[pl.ds(pl.multiple_of(other * share, share), share), :],
            dst_ref=out_ref.at[:, pl.ds(pl.multiple_of(own * DV, DV), DV)],
            send_sem=send.at[other],
            recv_sem=recv.at[own],
            device_id={"ctx": other // HK, "fsdp": other % HK},
            device_id_type=pl.DeviceIdType.MESH,
        )

    for at in range(block // share):
        other = step * (block // share) + at

        @pl.when(other != me)
        def _():
            leave(other).start()

        @pl.when(other == me)
        def _():
            pltpu.make_async_copy(
                held_out.at[pl.ds(pl.multiple_of(other * share, share), share), :],
                out_ref.at[:, pl.ds(pl.multiple_of(own * DV, DV), DV)],
                recv.at[own],
            ).start()

    @pl.when(step == pl.num_programs(0) - 1)
    def _():
        for other in range(peers):
            column = out_ref.at[:, pl.ds(other * DV, DV)]
            pltpu.make_async_copy(column, column, recv.at[other]).wait()

            @pl.when(other != me)
            def _():
                leave(other).wait_send()


def layer(hidden, weights, taps, scal, tail, entry, direct=False, interpret=False):
    tokens, width = hidden.shape
    full = lambda a: pl.BlockSpec(a.shape, lambda i: (0,) * a.ndim)
    scratch = [pltpu.VMEM((BLOCK + 8, 3 * DK), jnp.float32), pltpu.VMEM((DK, DV), jnp.float32)]
    params = dict(vmem_limit_bytes=48 * 1024 * 1024)
    if direct:
        peers = 2 * HK
        out_spec = pl.BlockSpec(memory_space=pl.ANY)
        out_shape = (tokens // peers, HV * DV)
        dma = pltpu.SemaphoreType.DMA
        scratch += [pltpu.VMEM((tokens, DV), jnp.bfloat16), dma((peers,)), dma((peers,))]
        params.update(collective_id=1, has_side_effects=True)
    else:
        out_spec = pl.BlockSpec((BLOCK, DV), lambda i: (i, 0))
        out_shape = (tokens, DV)
    return pl.pallas_call(
        layer_kernel,
        grid=(tokens // BLOCK,),
        in_specs=[pl.BlockSpec((BLOCK, width), lambda i: (i, 0))]
        + [full(a) for a in (weights, taps, scal, tail, entry)],
        out_specs=out_spec,
        out_shape=jax.ShapeDtypeStruct(out_shape, jnp.bfloat16),
        scratch_shapes=scratch,
        compiler_params=pltpu.CompilerParams(**params),
        interpret=interpret,
    )(hidden, weights, taps, scal, tail, entry)


def head_columns(array, own_qk, own_v):
    picks = (own_qk * DK, (HK + own_qk) * DK, 2 * HK * DK + own_v * DV)
    return jnp.concatenate([lax.dynamic_slice_in_dim(array, at, DK, 1) for at in picks], axis=1)


def ring_member(place, peers):
    late = place // (peers // 2)
    return 2 * place * (1 - late) + (2 * peers - 1 - 2 * place) * late


def exchange_kernel(
    hid_ref, shard_ref, gate_ref, all_ref, w_ref, ring_send, ring_recv, twin_send, twin_recv, local, w_send, w_recv, w_local
):
    g, c, f = lax.axis_index("groups"), lax.axis_index("ctx"), lax.axis_index("fsdp")
    peers = HK
    rows = hid_ref.shape[0]
    half = rows // 2
    place = (f // 2) * (1 - f % 2) + (peers - 1 - f // 2) * (f % 2)
    there = lambda cc, ff, gg=g: {"groups": gg, "ctx": cc, "fsdp": ff}
    barrier = pltpu.get_barrier_semaphore()
    for cc in range(2):
        for df in range(peers):
            if cc or df:
                pl.semaphore_signal(
                    barrier,
                    inc=1,
                    device_id=there((c + cc) % 2, (f + df) % peers),
                    device_id_type=pl.DeviceIdType.MESH,
                )
    for cc in range(2):
        pl.semaphore_signal(
            barrier, inc=1, device_id=there((c + cc) % 2, f, 1 - g), device_id_type=pl.DeviceIdType.MESH
        )
    pl.semaphore_wait(barrier, 2 * peers + 1)

    def remote(src, dst, send, recv, device):
        return pltpu.make_async_remote_copy(
            src_ref=src, dst_ref=dst, send_sem=send, recv_sem=recv, device_id=device, device_id_type=pl.DeviceIdType.MESH
        )

    def landing(member, start, size):
        return all_ref.at[pl.ds(pl.multiple_of((c * peers + member) * rows + start, half), size), :]

    def span(way, hop):
        return (0, rows) if hop < peers // 2 else ((0, half) if way == 0 else (half, half))

    def ring(way, hop):
        ahead = 1 if way == 0 else peers - 1
        target = ring_member((place + ahead) % peers, peers)
        origin = ring_member((place + (peers - ahead) * (hop - 1)) % peers, peers)
        start, size = span(way, hop)
        src = hid_ref.at[pl.ds(start, size), :] if hop == 1 else landing(origin, start, size)
        return remote(
            src, landing(origin, start, size), ring_send.at[way, hop - 1], ring_recv.at[way, hop - 1], there(c, target)
        )

    def twin(way, hop):
        ahead = 1 if way == 0 else peers - 1
        origin = ring_member((place + (peers - ahead) * hop) % peers, peers)
        block = landing(origin, *span(way, hop))
        at = 1 + way * (peers // 2) + hop - 1
        return remote(block, block, twin_send.at[at], twin_recv.at[at], there(1 - c, f))

    quarter = shard_ref.shape[0] // 4
    lines_qk = pl.ds(pl.multiple_of((2 * g + c) * quarter, quarter), quarter)
    lines_v = pl.ds(pl.multiple_of(2 * g * quarter, quarter), 2 * quarter)

    def weight(i, qk):
        if qk:
            d = (HK // 2) * (f % 2) + i
            src = shard_ref.at[lines_qk, pl.ds(i * DK, DK)]
            dst = w_ref.at[lines_qk, pl.ds(pl.multiple_of((f // 2) * DK, DK), DK)]
            sem = w_recv.at[f // 2]
        else:
            d = 2 * (f - 4) + i
            src = shard_ref.at[lines_v, pl.ds(pl.multiple_of((2 * i + c) * DK, DK), DK)]
            dst = w_ref.at[lines_v, pl.ds(2 * DK, DK)]
            sem = w_recv.at[2]
        return d, src, dst, sem

    def weights(finish):
        for qk, count in ((True, 4), (False, 2)):

            @pl.when((f < 4) if qk else (f >= 4))
            def _():
                for i in range(count):
                    d, src, dst, sem = weight(i, qk)

                    @pl.when(d != f)
                    def _():
                        far = remote(src, dst, w_send.at[i], sem, there(c, d))
                        far.wait_send() if finish else far.start()

                    if not finish:

                        @pl.when(d == f)
                        def _():
                            pltpu.make_async_copy(src, dst, sem).start()

    blocks = [w_ref.at[lines_qk, pl.ds(t * DK, DK)] for t in range(2)] + [w_ref.at[lines_v, pl.ds(2 * DK, DK)]]
    others = ((0, 1), (1, 0), (1, 1))

    def weight_shares():
        for t in range(3):
            for at, (dg, dc) in enumerate(others if t < 2 else others[1:2]):
                sem = 4 + 3 * t + at
                yield remote(blocks[t], blocks[t], w_send.at[sem], w_recv.at[sem], there((c + dc) % 2, f, (g + dg) % 2))

    weights(False)
    hops = peers // 2
    for way in range(2):
        ring(way, 1).start()
    first = remote(hid_ref, landing(f, 0, rows), twin_send.at[0], twin_recv.at[0], there(1 - c, f))
    first.start()
    own = pltpu.make_async_copy(hid_ref, landing(f, 0, rows), local)
    own.start()
    gate = pltpu.make_async_copy(gate_ref, w_ref.at[:, pl.ds(3 * DK, DK)], w_local)
    gate.start()
    for hop in range(1, hops + 1):
        for way in range(2):
            ring(way, hop).wait_recv()
            if hop < hops:
                ring(way, hop + 1).start()
            twin(way, hop).start()
        if hop == 1:
            for t in range(3):
                pltpu.make_async_copy(blocks[t], blocks[t], w_recv.at[t]).wait()
            for share in weight_shares():
                share.start()
    own.wait()
    gate.wait()
    first.wait()
    for share in weight_shares():
        share.wait()
    weights(True)
    for hop in range(1, hops + 1):
        for way in range(2):
            ring(way, hop).wait_send()
            twin(way, hop).wait()


def exchange(hidden_in, qkv_weight, gates):
    rows, width = hidden_in.shape
    anywhere = pl.BlockSpec(memory_space=pl.ANY)
    dma = pltpu.SemaphoreType.DMA
    return pl.pallas_call(
        exchange_kernel,
        in_specs=[anywhere] * 3,
        out_specs=[anywhere] * 2,
        out_shape=[
            jax.ShapeDtypeStruct((2 * HK * rows, width), jnp.bfloat16),
            jax.ShapeDtypeStruct((width, 4 * DK), jnp.bfloat16),
        ],
        scratch_shapes=[dma((2, HK // 2)), dma((2, HK // 2)), dma((HK + 1,)), dma((HK + 1,)), dma, dma((11,)), dma((11,)), dma],
        compiler_params=pltpu.CompilerParams(collective_id=0, has_side_effects=True),
    )(hidden_in, qkv_weight, gates)


def shards(
    hidden_in,
    qkv_weight,
    ab_weight,
    conv_weight,
    decay_rate,
    dt_bias,
    norm_gain,
    previous_tail,
    window_entry_state,
):
    c, f = lax.axis_index("ctx"), lax.axis_index("fsdp")
    own_qk = f % HK
    own = (HV // HK) * own_qk + c
    both = ("ctx", "fsdp")
    gates = jnp.stack(
        [lax.dynamic_index_in_dim(ab_weight, own, 1, False), lax.dynamic_index_in_dim(ab_weight, HV + own, 1, False)],
        axis=1,
    )
    gates = jnp.pad(gates, ((0, 0), (0, DK - 2)))
    direct = lax.axis_size("fsdp") == HK and lax.axis_size("groups") == 2
    if direct:
        hidden, weights = exchange(hidden_in, qkv_weight, gates)
    else:
        hidden = lax.all_gather(hidden_in, both, axis=0, tiled=True)
        columns = head_columns(lax.all_gather(qkv_weight, "fsdp", axis=1, tiled=True), own_qk, own)
        weights = jnp.concatenate([columns, gates], axis=1)
    taps = jnp.pad(head_columns(conv_weight, own_qk, own), ((0, 4), (0, 0)))
    tail = jnp.pad(head_columns(previous_tail, own_qk, own).astype(jnp.float32), ((5, 0), (0, 0)))
    take = lambda a: jnp.full((1, DV), lax.dynamic_index_in_dim(a, own, 0, False))
    scal = jnp.concatenate(
        [take(decay_rate), take(dt_bias), norm_gain[None, :], jnp.zeros((5, DV), jnp.float32)], axis=0
    )
    entry = lax.dynamic_index_in_dim(window_entry_state, own, 0, False)
    result = layer(hidden, weights, taps, scal, tail, entry, direct)
    if direct:
        return result
    peers = lax.axis_size("ctx") * lax.axis_size("fsdp")
    rows = result.reshape(peers, result.shape[0] // peers, DV)
    swapped = lax.all_to_all(rows, both, 0, 0)
    swapped = swapped.reshape(lax.axis_size("ctx"), lax.axis_size("fsdp"), rows.shape[1], DV)[:, :HK]
    return jnp.transpose(swapped, (2, 1, 0, 3)).reshape(rows.shape[1], HV * DV)


def solution(mesh):
    placed = (
        P(("groups", "ctx", "fsdp"), None),
        P(None, "fsdp"),
        P(),
        P(),
        P(),
        P(),
        P(),
        P("groups", None),
        P("groups", None, None),
    )
    return jax.shard_map(
        shards,
        mesh=mesh,
        in_specs=placed,
        out_specs=P(("groups", "ctx", "fsdp"), None),
        check_vma=False,
    )
```

```python
import jax
import jax.numpy as jnp
from jax import lax
from jax.experimental import pallas as pl
from jax.experimental.pallas import tpu as pltpu
from jax.sharding import PartitionSpec as P

HK = 8
HV = 16
DK = 128
DV = 128
BLOCK = 1024
CHUNK = 128
BASE = 32


def mm(a, b):
    return jnp.dot(a.astype(jnp.bfloat16), b.astype(jnp.bfloat16), preferred_element_type=jnp.float32)


def mm_nt(a, b):
    return lax.dot_general(
        a.astype(jnp.bfloat16),
        b.astype(jnp.bfloat16),
        (((1,), (1,)), ((), ())),
        preferred_element_type=jnp.float32,
    )


def mm_tn(a, b):
    return lax.dot_general(
        a.astype(jnp.bfloat16),
        b.astype(jnp.bfloat16),
        (((0,), (0,)), ((), ())),
        preferred_element_type=jnp.float32,
    )


def unit_lower_inverses(parts, row, col):
    eye = jnp.where(row == col, 1.0, 0.0)
    near = (row // BASE) == (col // BASE)
    powers = [jnp.where(near, a, 0.0) for a in parts]
    inverses = [eye - p for p in powers]
    reach = 2
    while reach < BASE:
        powers = [mm(p, p) for p in powers]
        inverses = [x + mm(x, p) for x, p in zip(inverses, powers)]
        reach *= 2
    size = BASE
    while size < CHUNK:
        joined = ((row // (2 * size)) == (col // (2 * size))) & ((row // size) != (col // size))
        sides = [mm(x, jnp.where(joined, a, 0.0)) for x, a in zip(inverses, parts)]
        inverses = [x - mm(y, x) for x, y in zip(inverses, sides)]
        size *= 2
    return inverses


def layer_kernel(hid_ref, w_ref, taps_ref, scal_ref, tail_ref, entry_ref, out_ref, buf, state, *sending):
    step = pl.program_id(0)
    if sending:
        held_out, send, recv = sending
        c, f = lax.axis_index("ctx"), lax.axis_index("fsdp")
        me, peers = c * HK + f, 2 * HK
        own = 2 * f + c
        share = out_ref.shape[0]
        barrier = pltpu.get_barrier_semaphore()

        @pl.when(step == 0)
        def _():
            for away in range(1, peers):
                other = (me + away) % peers
                pl.semaphore_signal(
                    barrier,
                    inc=1,
                    device_id={"ctx": other // HK, "fsdp": other % HK},
                    device_id_type=pl.DeviceIdType.MESH,
                )

    @pl.when(step == 0)
    def _():
        state[...] = entry_ref[...]
        buf[0:8, :] = tail_ref[...]

    block = hid_ref.shape[0]
    wide = 3 * DK
    product = jnp.dot(hid_ref[...], w_ref[...], preferred_element_type=jnp.float32)
    buf[8 : 8 + block, :] = product[:, :wide].astype(jnp.bfloat16).astype(jnp.float32)
    summed = taps_ref[0:1, :] * buf[5 : 5 + block, :]
    for j in range(1, 4):
        summed = summed + taps_ref[j : j + 1, :] * buf[5 + j : 5 + j + block, :]
    buf[0:8, :] = buf[block : block + 8, :]
    conv = summed / (1.0 + jnp.exp(-summed))
    q = conv[:, :DK]
    k = conv[:, DK : 2 * DK]
    v = conv[:, 2 * DK :]
    q = q * (lax.rsqrt(jnp.sum(q * q, axis=-1, keepdims=True) + 1e-06) * DK ** (-0.5))
    k = k * lax.rsqrt(jnp.sum(k * k, axis=-1, keepdims=True) + 1e-06)

    spans = block // CHUNK
    row = lax.broadcasted_iota(jnp.int32, (CHUNK, CHUNK), 0)
    col = lax.broadcasted_iota(jnp.int32, (CHUNK, CHUNK), 1)
    low = row >= col
    upper = jnp.where(row <= col, 1.0, 0.0)
    logits = jnp.transpose(product[:, wide:], (1, 0))[0:8, :]
    shifted_logit = logits[0:1, :] + scal_ref[1:2, 0:1]
    softplus = jnp.maximum(shifted_logit, 0.0) + jnp.log1p(jnp.exp(-jnp.abs(shifted_logit)))
    logdecay = -scal_ref[0:1, 0:1] * softplus
    rate = 1.0 / (1.0 + jnp.exp(-logits[1:2, :]))
    decays = jnp.concatenate(
        [logdecay[:, i * CHUNK : (i + 1) * CHUNK] for i in range(spans)]
        + [jnp.zeros((8 - spans, CHUNK), jnp.float32)] * (1 if spans < 8 else 0),
        axis=0,
    )
    sums = jnp.dot(decays, upper, precision=lax.Precision.HIGHEST, preferred_element_type=jnp.float32)

    ks, qs, parts, scores, rights, ends, tails = [], [], [], [], [], [], []
    for i in range(spans):
        part = slice(i * CHUNK, (i + 1) * CHUNK)
        ki, qi, vi = k[part], q[part], v[part]
        cs = sums[i : i + 1, :]
        beta = rate[:, part]
        end = cs[:, CHUNK - 1 : CHUNK]
        growth = jnp.exp(cs)
        rows = jnp.concatenate(
            [cs, beta, growth, beta * growth, jnp.exp(end - cs), jnp.zeros((CHUNK - 5, CHUNK), jnp.float32)], axis=0
        )
        cols = jnp.transpose(rows, (1, 0))
        gap = cols[:, 0:1] - cs
        factor = jnp.where(low, jnp.exp(jnp.where(low, gap, 0.0)), 0.0)
        both = mm_nt(jnp.concatenate([ki, qi], axis=0), ki)
        parts.append(jnp.where(row > col, cols[:, 1:2] * both[:CHUNK] * factor, 0.0))
        scores.append(both[CHUNK:] * factor)
        rights.append(jnp.concatenate([cols[:, 1:2] * vi, cols[:, 3:4] * ki], axis=1))
        qs.append(cols[:, 2:3] * qi)
        ks.append(ki * cols[:, 4:5])
        ends.append(jnp.exp(end))
    inverses = unit_lower_inverses(parts, row, col)
    solved = [mm(x, r) for x, r in zip(inverses, rights)]

    held = state[...]
    for i in range(spans):
        both = mm(jnp.concatenate([solved[i][:, DV:], qs[i]], axis=0), held)
        fresh = solved[i][:, :DV] - both[:CHUNK]
        result = both[CHUNK:] + mm(scores[i], fresh)
        held = ends[i] * held + mm_tn(ks[i], fresh)
        mean_square = jnp.mean(result * result, axis=-1, keepdims=True)
        normed = (result * lax.rsqrt(mean_square + 1e-06) * scal_ref[2:3, :]).astype(jnp.bfloat16)
        if sending:
            held_out[pl.ds(pl.multiple_of(step * block + i * CHUNK, CHUNK), CHUNK), :] = normed
        else:
            out_ref[i * CHUNK : (i + 1) * CHUNK, :] = normed
    state[...] = held
    if not sending:
        return

    @pl.when(step == 0)
    def _():
        pl.semaphore_wait(barrier, peers - 1)

    def leave(other):
        return pltpu.make_async_remote_copy(
            src_ref=held_out.at[pl.ds(pl.multiple_of(other * share, share), share), :],
            dst_ref=out_ref.at[:, pl.ds(pl.multiple_of(own * DV, DV), DV)],
            send_sem=send.at[other],
            recv_sem=recv.at[own],
            device_id={"ctx": other // HK, "fsdp": other % HK},
            device_id_type=pl.DeviceIdType.MESH,
        )

    for at in range(block // share):
        other = step * (block // share) + at

        @pl.when(other != me)
        def _():
            leave(other).start()

        @pl.when(other == me)
        def _():
            pltpu.make_async_copy(
                held_out.at[pl.ds(pl.multiple_of(other * share, share), share), :],
                out_ref.at[:, pl.ds(pl.multiple_of(own * DV, DV), DV)],
                recv.at[own],
            ).start()

    @pl.when(step == pl.num_programs(0) - 1)
    def _():
        for other in range(peers):
            column = out_ref.at[:, pl.ds(other * DV, DV)]
            pltpu.make_async_copy(column, column, recv.at[other]).wait()

            @pl.when(other != me)
            def _():
                leave(other).wait_send()


def layer(hidden, weights, taps, scal, tail, entry, direct=False, interpret=False):
    tokens, width = hidden.shape
    full = lambda a: pl.BlockSpec(a.shape, lambda i: (0,) * a.ndim)
    scratch = [pltpu.VMEM((BLOCK + 8, 3 * DK), jnp.float32), pltpu.VMEM((DK, DV), jnp.float32)]
    params = dict(vmem_limit_bytes=48 * 1024 * 1024)
    if direct:
        peers = 2 * HK
        out_spec = pl.BlockSpec(memory_space=pl.ANY)
        out_shape = (tokens // peers, HV * DV)
        dma = pltpu.SemaphoreType.DMA
        scratch += [pltpu.VMEM((tokens, DV), jnp.bfloat16), dma((peers,)), dma((peers,))]
        params.update(collective_id=1, has_side_effects=True)
    else:
        out_spec = pl.BlockSpec((BLOCK, DV), lambda i: (i, 0))
        out_shape = (tokens, DV)
    return pl.pallas_call(
        layer_kernel,
        grid=(tokens // BLOCK,),
        in_specs=[pl.BlockSpec((BLOCK, width), lambda i: (i, 0))]
        + [full(a) for a in (weights, taps, scal, tail, entry)],
        out_specs=out_spec,
        out_shape=jax.ShapeDtypeStruct(out_shape, jnp.bfloat16),
        scratch_shapes=scratch,
        compiler_params=pltpu.CompilerParams(**params),
        interpret=interpret,
    )(hidden, weights, taps, scal, tail, entry)


def head_columns(array, own_qk, own_v):
    picks = (own_qk * DK, (HK + own_qk) * DK, 2 * HK * DK + own_v * DV)
    return jnp.concatenate([lax.dynamic_slice_in_dim(array, at, DK, 1) for at in picks], axis=1)


def ring_member(place, peers):
    late = place // (peers // 2)
    return 2 * place * (1 - late) + (2 * peers - 1 - 2 * place) * late


def exchange_kernel(
    hid_ref, shard_ref, gate_ref, all_ref, w_ref, ring_send, ring_recv, twin_send, twin_recv, local, w_send, w_recv, w_local
):
    g, c, f = lax.axis_index("groups"), lax.axis_index("ctx"), lax.axis_index("fsdp")
    peers = HK
    rows = hid_ref.shape[0]
    half = rows // 2
    place = (f // 2) * (1 - f % 2) + (peers - 1 - f // 2) * (f % 2)
    there = lambda cc, ff, gg=g: {"groups": gg, "ctx": cc, "fsdp": ff}
    barrier = pltpu.get_barrier_semaphore()
    for cc in range(2):
        for df in range(peers):
            if cc or df:
                pl.semaphore_signal(
                    barrier,
                    inc=1,
                    device_id=there((c + cc) % 2, (f + df) % peers),
                    device_id_type=pl.DeviceIdType.MESH,
                )
    for cc in range(2):
        pl.semaphore_signal(
            barrier, inc=1, device_id=there((c + cc) % 2, f, 1 - g), device_id_type=pl.DeviceIdType.MESH
        )
    pl.semaphore_wait(barrier, 2 * peers + 1)

    def remote(src, dst, send, recv, device):
        return pltpu.make_async_remote_copy(
            src_ref=src, dst_ref=dst, send_sem=send, recv_sem=recv, device_id=device, device_id_type=pl.DeviceIdType.MESH
        )

    def landing(member, start, size):
        return all_ref.at[pl.ds(pl.multiple_of((c * peers + member) * rows + start, half), size), :]

    def span(way, hop):
        return (0, rows) if hop < peers // 2 else ((0, half) if way == 0 else (half, half))

    def ring(way, hop):
        ahead = 1 if way == 0 else peers - 1
        target = ring_member((place + ahead) % peers, peers)
        origin = ring_member((place + (peers - ahead) * (hop - 1)) % peers, peers)
        start, size = span(way, hop)
        src = hid_ref.at[pl.ds(start, size), :] if hop == 1 else landing(origin, start, size)
        return remote(
            src, landing(origin, start, size), ring_send.at[way, hop - 1], ring_recv.at[way, hop - 1], there(c, target)
        )

    def twin(way, hop):
        ahead = 1 if way == 0 else peers - 1
        origin = ring_member((place + (peers - ahead) * hop) % peers, peers)
        block = landing(origin, *span(way, hop))
        at = 1 + way * (peers // 2) + hop - 1
        return remote(block, block, twin_send.at[at], twin_recv.at[at], there(1 - c, f))

    quarter = shard_ref.shape[0] // 4
    lines_qk = pl.ds(pl.multiple_of((2 * g + c) * quarter, quarter), quarter)
    lines_v = pl.ds(pl.multiple_of(2 * g * quarter, quarter), 2 * quarter)

    def weight(i, qk):
        if qk:
            d = (HK // 2) * (f % 2) + i
            src = shard_ref.at[lines_qk, pl.ds(i * DK, DK)]
            dst = w_ref.at[lines_qk, pl.ds(pl.multiple_of((f // 2) * DK, DK), DK)]
            sem = w_recv.at[f // 2]
        else:
            d = 2 * (f - 4) + i
            src = shard_ref.at[lines_v, pl.ds(pl.multiple_of((2 * i + c) * DK, DK), DK)]
            dst = w_ref.at[lines_v, pl.ds(2 * DK, DK)]
            sem = w_recv.at[2]
        return d, src, dst, sem

    def weights(finish):
        for qk, count in ((True, 4), (False, 2)):

            @pl.when((f < 4) if qk else (f >= 4))
            def _():
                for i in range(count):
                    d, src, dst, sem = weight(i, qk)

                    @pl.when(d != f)
                    def _():
                        far = remote(src, dst, w_send.at[i], sem, there(c, d))
                        far.wait_send() if finish else far.start()

                    if not finish:

                        @pl.when(d == f)
                        def _():
                            pltpu.make_async_copy(src, dst, sem).start()

    blocks = [w_ref.at[lines_qk, pl.ds(t * DK, DK)] for t in range(2)] + [w_ref.at[lines_v, pl.ds(2 * DK, DK)]]
    others = ((0, 1), (1, 0), (1, 1))

    def weight_shares():
        for t in range(3):
            for at, (dg, dc) in enumerate(others if t < 2 else others[1:2]):
                sem = 4 + 3 * t + at
                yield remote(blocks[t], blocks[t], w_send.at[sem], w_recv.at[sem], there((c + dc) % 2, f, (g + dg) % 2))

    weights(False)
    hops = peers // 2
    for way in range(2):
        ring(way, 1).start()
    first = remote(hid_ref, landing(f, 0, rows), twin_send.at[0], twin_recv.at[0], there(1 - c, f))
    first.start()
    own = pltpu.make_async_copy(hid_ref, landing(f, 0, rows), local)
    own.start()
    gate = pltpu.make_async_copy(gate_ref, w_ref.at[:, pl.ds(3 * DK, DK)], w_local)
    gate.start()
    for hop in range(1, hops + 1):
        for way in range(2):
            ring(way, hop).wait_recv()
            if hop < hops:
                ring(way, hop + 1).start()
            twin(way, hop).start()
        if hop == 1:
            for t in range(3):
                pltpu.make_async_copy(blocks[t], blocks[t], w_recv.at[t]).wait()
            for share in weight_shares():
                share.start()
    own.wait()
    gate.wait()
    first.wait()
    for share in weight_shares():
        share.wait()
    weights(True)
    for hop in range(1, hops + 1):
        for way in range(2):
            ring(way, hop).wait_send()
            twin(way, hop).wait()


def exchange(hidden_in, qkv_weight, gates):
    rows, width = hidden_in.shape
    anywhere = pl.BlockSpec(memory_space=pl.ANY)
    dma = pltpu.SemaphoreType.DMA
    return pl.pallas_call(
        exchange_kernel,
        in_specs=[anywhere] * 3,
        out_specs=[anywhere] * 2,
        out_shape=[
            jax.ShapeDtypeStruct((2 * HK * rows, width), jnp.bfloat16),
            jax.ShapeDtypeStruct((width, 4 * DK), jnp.bfloat16),
        ],
        scratch_shapes=[dma((2, HK // 2)), dma((2, HK // 2)), dma((HK + 1,)), dma((HK + 1,)), dma, dma((11,)), dma((11,)), dma],
        compiler_params=pltpu.CompilerParams(collective_id=0, has_side_effects=True),
    )(hidden_in, qkv_weight, gates)


def shards(
    hidden_in,
    qkv_weight,
    ab_weight,
    conv_weight,
    decay_rate,
    dt_bias,
    norm_gain,
    previous_tail,
    window_entry_state,
):
    c, f = lax.axis_index("ctx"), lax.axis_index("fsdp")
    own_qk = f % HK
    own = (HV // HK) * own_qk + c
    both = ("ctx", "fsdp")
    line = lax.broadcasted_iota(jnp.int32, (2 * HV, DK), 0)
    column = lax.broadcasted_iota(jnp.int32, (2 * HV, DK), 1)
    chosen = (line == own + HV * column) & (column < 2)
    gates = jnp.dot(ab_weight, chosen.astype(jnp.bfloat16), preferred_element_type=jnp.float32).astype(jnp.bfloat16)
    direct = lax.axis_size("fsdp") == HK and lax.axis_size("groups") == 2
    if direct:
        hidden, weights = exchange(hidden_in, qkv_weight, gates)
    else:
        hidden = lax.all_gather(hidden_in, both, axis=0, tiled=True)
        columns = head_columns(lax.all_gather(qkv_weight, "fsdp", axis=1, tiled=True), own_qk, own)
        weights = jnp.concatenate([columns, gates], axis=1)
    taps = jnp.pad(head_columns(conv_weight, own_qk, own), ((0, 4), (0, 0)))
    tail = jnp.pad(head_columns(previous_tail, own_qk, own).astype(jnp.float32), ((5, 0), (0, 0)))
    take = lambda a: jnp.full((1, DV), lax.dynamic_index_in_dim(a, own, 0, False))
    scal = jnp.concatenate(
        [take(decay_rate), take(dt_bias), norm_gain[None, :], jnp.zeros((5, DV), jnp.float32)], axis=0
    )
    entry = lax.dynamic_index_in_dim(window_entry_state, own, 0, False)
    result = layer(hidden, weights, taps, scal, tail, entry, direct)
    if direct:
        return result
    peers = lax.axis_size("ctx") * lax.axis_size("fsdp")
    rows = result.reshape(peers, result.shape[0] // peers, DV)
    swapped = lax.all_to_all(rows, both, 0, 0)
    swapped = swapped.reshape(lax.axis_size("ctx"), lax.axis_size("fsdp"), rows.shape[1], DV)[:, :HK]
    return jnp.transpose(swapped, (2, 1, 0, 3)).reshape(rows.shape[1], HV * DV)


def solution(mesh):
    placed = (
        P(("groups", "ctx", "fsdp"), None),
        P(None, "fsdp"),
        P(),
        P(),
        P(),
        P(),
        P(),
        P("groups", None),
        P("groups", None, None),
    )
    return jax.shard_map(
        shards,
        mesh=mesh,
        in_specs=placed,
        out_specs=P(("groups", "ctx", "fsdp"), None),
        check_vma=False,
    )
```
